32 devices in a mesh: grp: 2 (over x), row: 8 (over z, y), col: 2 (over core).
Axes of the slice: x: 2, y: 2, z: 4, core: 2. Of those that a mesh axis runs over, the one named last changes fastest.
Arguments:
- activations: bfloat16 [128, 8192], P(('grp', 'row', 'col')), parts along dimension 0, may hold values from -2 to 2
- out_grad: bfloat16 [128, 49152], P(('grp', 'row'), 'col'), parts along dimension 0, may hold values from -6 to 6
- weights: bfloat16 [64, 256, 128, 128], P('row', 'col'), may hold values from -0.0390625 to 0.0390625
- counts: int32 [64, 2], P('row', 'col'), may hold values from 64 to 128, as said below
- col_index: int32 [64, 256], P('row', 'col'), may hold values from 0 to 383, as said below
Outputs:
- grad_input: bfloat16 [128, 8192], P(('grp', 'row', 'col')), parts along dimension 0
- grad_weight: bfloat16 [128, 256, 128, 128], P(('grp', 'row'), 'col'), parts along dimension 0
The draws below stay inside these ranges and needn't reach their ends.
There are 2 independent parts, one for each index of `grp`. The reference program is written for one: setup_inputs(seed, part) draws one part's arguments, and reference() takes and returns one part's arrays. A program takes and returns all parts, laid end to end along the dimension named above; an argument that names none is the same for every part. Nothing has to cross between parts.
Inputs may be any that keep to these rules, and one draw needn't show every extreme that they name: `counts`: each entry lies between 64 and 128; in every draw at least one block row has exactly 128 kept blocks in one half. `col_index`: slots h * 128 to (h + 1) * 128 - 1 of a block row hold block columns h * 192 to (h + 1) * 192 - 1; its first counts[i, h] slots hold distinct columns in ascending order, and the remaining slots repeat the first of them.
All inputs are finite; a program needn't handle non-finite values.
Results may differ from the reference program's by a relative error of at most 0.001.
Values may be sent and summed in bfloat16 or wider, within the bound.
A program may use at most 192 MiB of HBM per device.

```python
import jax
import jax.numpy as jnp
from jax import lax

D = 8192
FF = 49152
BLK = 128
CAP = 128
TOKENS = 64
KBR = 64
NBC = 192
N_COL = 2


def block_lists(key):
    count_key, order_key, half_key, row_key = jax.random.split(key, 4)
    counts = jax.random.randint(count_key, (KBR, N_COL), CAP // 2, CAP + 1)
    forced_row = jax.random.randint(row_key, (), 0, KBR)
    forced_half = jax.random.randint(half_key, (), 0, N_COL)
    row_ids = lax_iota((KBR, N_COL), 0)
    half_ids = lax_iota((KBR, N_COL), 1)
    counts = jnp.where((row_ids == forced_row) & (half_ids == forced_half), CAP, counts)
    scores = jax.random.randint(order_key, (KBR, N_COL, NBC), 0, 1 << 20) * NBC + lax_iota((KBR, N_COL, NBC), 2)
    order = jnp.argsort(scores, axis=-1)[:, :, :CAP].astype(jnp.int32)
    slot_ids = lax_iota((KBR, N_COL, CAP), 2)
    alive = slot_ids < counts[:, :, None]
    keyed = jnp.where(alive, order, NBC + slot_ids)
    ordered = jnp.sort(keyed, axis=-1)
    padded = jnp.where(alive, ordered, ordered[:, :, :1])
    index = padded + half_ids[:, :, None] * NBC
    return (counts.astype(jnp.int32), index.reshape(KBR, N_COL * CAP).astype(jnp.int32))


def lax_iota(shape, axis):
    return jax.lax.broadcasted_iota(jnp.int32, shape, axis)


def draw_counts(key, part):
    shared = block_lists(key)
    return shared[0]


def draw_col_index(key, part):
    shared = block_lists(key)
    return shared[1]


def steps_of(key, dims, pieces, smallest, top_value):
    loudness = 1.0
    for position, blocks in pieces:
        heights = jax.random.uniform(jax.random.fold_in(jax.random.fold_in(key, 6), position), (blocks,), jnp.float32, smallest / len(pieces), top_value / len(pieces))
        loudness = loudness * jnp.repeat(jnp.exp(heights), dims[position] // blocks).reshape((-1,) + (1,) * (len(dims) - 1 - position))
    return loudness


def noise(key, extent, scale, limit, pieces=(), held_as=jnp.bfloat16):
    drawn = jax.random.normal(key, extent, jnp.float32) * scale
    if len(pieces) > 0:
        drawn = steps_of(key, extent, pieces, -0.22, 0.18) * drawn
    return jnp.clip(drawn, min=-limit, max=limit).astype(held_as)


def setup_inputs(seed: int = 0, part: int = 0) -> dict:
    key_of = jax.random.split(jax.random.key(seed), 6)
    own_keys = jax.random.split(jax.random.fold_in(key_of[5], part), 6)
    return {
        "activations": noise(own_keys[0], (TOKENS, D), (TOKENS ** -0.5), 2.0, ((0, 16),)),
        "out_grad": noise(own_keys[1], (TOKENS, FF), 1.0, 6.0, ((0, 8), (1, 2))),
        "weights": noise(key_of[2], (KBR, N_COL * CAP, BLK, BLK), (FF // 2) ** -0.5, 0.0390625, ((0, 8), (1, 2))),
        "counts": draw_counts(jax.random.fold_in(key_of[5], 71), part),
        "col_index": draw_col_index(jax.random.fold_in(key_of[5], 71), part),
    }


def reference(activations, out_grad, weights, counts, col_index):
    grad_blocks = out_grad.reshape(TOKENS, FF // BLK, BLK)
    input_blocks = activations.reshape(TOKENS, KBR, BLK).transpose(1, 0, 2)
    slot_ids = jnp.arange(N_COL * CAP, dtype=jnp.int32)
    half_of = slot_ids // CAP
    within = slot_ids % CAP

    def one_row(items):
        x_row, w_row, row_counts, row_index = items
        alive = within < row_counts[half_of]
        panels = jnp.take(grad_blocks, row_index, axis=1).astype(jnp.float32)
        masked = jnp.where(alive[:, None, None], w_row.astype(jnp.float32), jnp.float32(0.0))
        grad_w = jnp.einsum("tk,tsn->skn", x_row.astype(jnp.float32), panels)
        grad_w = jnp.where(alive[:, None, None], grad_w, jnp.float32(0.0)).astype(jnp.bfloat16)
        grad_x = jnp.einsum("tsn,skn->tk", panels, masked)
        return grad_x, grad_w

    grad_x, grad_weight = lax.map(one_row, (input_blocks, weights, counts, col_index))
    grad_input = grad_x.transpose(1, 0, 2).reshape(TOKENS, D).astype(jnp.bfloat16)
    return grad_input, grad_weight
```

```python
import functools

import jax
import jax.numpy as jnp
from jax import lax
from jax.experimental import pallas as pl
from jax.experimental.pallas import tpu as pltpu
from jax.sharding import PartitionSpec as P

MESH = pl.DeviceIdType.MESH
GROUP = 8
AHEAD = 2


def gather_kernel(
    rows,
    chunks,
    inv_ref,
    og_ref,
    xs_ref,
    w_hbm,
    nat_ref,
    xo_ref,
    go_ref,
    raw,
    wbuf,
    acc,
    xr,
    q_send,
    q_recv,
    q_mine,
    obuf,
    orecv,
    w_sem,
    ring_send,
    ring_recv,
    x_send,
    x_recv,
    q_sems,
    o_send,
    o_recv,
):
    half = rows // 2
    here = acc.shape[0]
    slots = w_hbm.shape[0]
    blk = w_hbm.shape[-1]
    tok = og_ref.shape[0]
    tokens = rows * tok
    pairs = raw.shape[1] // chunks
    cols = pairs * 2
    peers = rows * 2
    row = lax.axis_index("row")
    col = lax.axis_index("col")
    me = row * 2 + col
    odd = row % 2
    pos = (1 - odd) * (row // 2) + odd * (rows - 1 - row // 2)

    def row_at(p):
        p = (p + 2 * rows) % rows
        hi = p // half
        return (1 - hi) * (2 * p) + hi * (2 * (rows - 1 - p) + 1)

    barrier = pltpu.get_barrier_semaphore()

    def greet(d, _):
        peer = (me + d) % peers
        pl.semaphore_signal(
            barrier, inc=1, device_id={"row": peer // 2, "col": peer % 2}, device_id_type=MESH
        )
        return 0

    lax.fori_loop(1, peers, greet, 0)
    w_copy = pltpu.make_async_copy(w_hbm, wbuf.at[pl.ds(0, slots)], w_sem)
    w_copy.start()

    def lay_out(q, _):
        both = og_ref[:, pl.ds(pl.multiple_of(q * 2 * blk, 2 * blk), 2 * blk)].astype(jnp.float32)
        raw[row, q] = jnp.concatenate([both[:, :blk], both[:, blk:]], axis=0).astype(raw.dtype)
        return 0

    lax.fori_loop(0, raw.shape[1], lay_out, 0, unroll=4)
    pl.semaphore_wait(barrier, peers - 1)

    def ring_copy(d, k, c):
        origin = row_at(pos - k) if d == 0 else row_at(pos + k)
        target = row_at(pos + 1) if d == 0 else row_at(pos - 1)
        part = raw.at[origin, pl.ds(c * pairs, pairs)]
        return pltpu.make_async_remote_copy(
            src_ref=part,
            dst_ref=part,
            send_sem=ring_send.at[d, k, c],
            recv_sem=ring_recv.at[d, k, c],
            device_id={"row": target},
            device_id_type=MESH,
        )

    def ring_arrival(d, k, c):
        origin = row_at(pos - 1 - k) if d == 0 else row_at(pos + 1 + k)
        target = row_at(pos + 1) if d == 0 else row_at(pos - 1)
        part = raw.at[origin, pl.ds(c * pairs, pairs)]
        return pltpu.make_async_remote_copy(
            src_ref=part,
            dst_ref=part,
            send_sem=ring_send.at[d, k, c],
            recv_sem=ring_recv.at[d, k, c],
            device_id={"row": target},
            device_id_type=MESH,
        )

    def x_copy(d):
        peer = (me + d) % peers
        return pltpu.make_async_remote_copy(
            src_ref=xs_ref.at[peer // 2],
            dst_ref=xr.at[me],
            send_sem=x_send.at[d],
            recv_sem=x_recv.at[d],
            device_id={"row": peer // 2, "col": peer % 2},
            device_id_type=MESH,
        )

    def x_arrival(d):
        peer = (me + peers - d) % peers
        return pltpu.make_async_remote_copy(
            src_ref=xs_ref.at[peer // 2],
            dst_ref=xr.at[peer],
            send_sem=x_send.at[d],
            recv_sem=x_recv.at[d],
            device_id={"row": peer // 2, "col": peer % 2},
            device_id_type=MESH,
        )

    for c in range(min(AHEAD, chunks)):
        for d in (0, 1):
            ring_copy(d, 0, c).start()

    def send_x(d, _):
        x_copy(d).start()
        return 0

    lax.fori_loop(1, peers, send_x, 0)
    xr[me] = xs_ref[row]
    wbuf[slots] = jnp.zeros((blk, blk), wbuf.dtype)
    acc[...] = jnp.zeros_like(acc)

    def hop(t, k):
        c = t - k
        for d in (0, 1):
            ok = (c >= 0) & (c < chunks)
            if k == half - 1:
                ok = ok & (c % 2 == d)

            @pl.when(ok)
            def _():
                ring_arrival(d, k - 1, c).wait_recv()
                ring_copy(d, k, c).start()

    def compute(c):
        def natural(j, _):
            q = c * pairs + j
            both = raw[:, q].astype(jnp.float32).reshape(rows, 2, tok, blk)
            nat_ref[2 * q] = both[:, 0].reshape(tokens, blk).astype(nat_ref.dtype)
            nat_ref[2 * q + 1] = both[:, 1].reshape(tokens, blk).astype(nat_ref.dtype)
            return 0

        lax.fori_loop(0, pairs, natural, 0, unroll=2)

        def group(g, _):
            first = c * cols + g * GROUP
            panel = jnp.concatenate([nat_ref[first + m] for m in range(GROUP)], axis=1)
            for i in range(here):
                blocks = jnp.concatenate(
                    [wbuf[inv_ref[i, first + m]] for m in range(GROUP)], axis=1
                )
                acc[i] += lax.dot_general(
                    blocks, panel, (((1,), (1,)), ((), ())), preferred_element_type=jnp.float32
                )
            return 0

        lax.fori_loop(0, cols // GROUP, group, 0)

    def tick(t, _):
        @pl.when(t + AHEAD < chunks)
        def _():
            for d in (0, 1):
                ring_copy(d, 0, t + AHEAD).start()

        if half > 1:
            hop(t, 1)
        for k in range(half - 1, 1, -1):
            hop(t, k)

        @pl.when(t >= half)
        def _():
            c = t - half

            @pl.when(c == 0)
            def _():
                w_copy.wait()

            for d in (0, 1):
                @pl.when(c % 2 == d)
                def _():
                    ring_arrival(d, half - 1, c).wait_recv()
                    ring_arrival(1 - d, half - 2, c).wait_recv()

            compute(c)

        return 0

    lax.fori_loop(0, chunks + half, tick, 0)

    below = lax.broadcasted_iota(jnp.int32, (rows, 8, blk), 1) < 4
    first_core = (lax.broadcasted_iota(jnp.int32, (rows, 8, blk), 1) * 0 + col) == 0
    zero = jnp.zeros((rows, 8, blk), jnp.float32)

    def tile(i):
        if i >= here:
            return zero
        return jnp.transpose(acc[i], (1, 0)).reshape(rows, tok, blk)

    for i2 in range(q_send.shape[1]):
        a, b = tile(2 * i2), tile(2 * i2 + 1)
        for_first = jnp.where(below, a, pltpu.roll(b, 4, 1))
        for_second = jnp.where(below, pltpu.roll(a, 4, 1), b)
        q_mine[:, i2] = jnp.where(first_core, for_first, for_second)
        q_send[:, i2] = jnp.where(first_core, for_second, for_first)

    swap = pltpu.make_async_remote_copy(
        src_ref=q_send,
        dst_ref=q_recv,
        send_sem=q_sems.at[0],
        recv_sem=q_sems.at[1],
        device_id={"col": 1 - col},
        device_id_type=MESH,
    )
    swap.start()

    def wait_x(d, _):
        x_arrival(d).wait_recv()
        x_copy(d).wait_send()
        return 0

    lax.fori_loop(1, peers, wait_x, 0)
    xo_ref[...] = xr[...]

    def wait_ring(c, _):
        for k in range(half):
            for d in (0, 1):
                if k == half - 1:

                    @pl.when(c % 2 == d)
                    def _():
                        ring_copy(d, k, c).wait_send()

                else:
                    ring_copy(d, k, c).wait_send()
        return 0

    lax.fori_loop(0, chunks, wait_ring, 0)
    swap.wait()
    total = q_mine[...] + q_recv[...]
    obuf[...] = total.reshape(obuf.shape).astype(obuf.dtype)

    def o_copy(d):
        peer = (row + d) % rows
        return pltpu.make_async_remote_copy(
            src_ref=obuf.at[peer],
            dst_ref=orecv.at[row],
            send_sem=o_send.at[d],
            recv_sem=o_recv.at[d],
            device_id={"row": peer},
            device_id_type=MESH,
        )

    def o_arrival(d):
        peer = (row + rows - d) % rows
        return pltpu.make_async_remote_copy(
            src_ref=obuf.at[peer],
            dst_ref=orecv.at[peer],
            send_sem=o_send.at[d],
            recv_sem=o_recv.at[d],
            device_id={"row": peer},
            device_id_type=MESH,
        )

    def send_o(d, _):
        o_copy(d).start()
        return 0

    def wait_o(d, _):
        o_arrival(d).wait_recv()
        o_copy(d).wait_send()
        return 0

    lax.fori_loop(1, rows, send_o, 0)
    orecv[row] = obuf[row]
    lax.fori_loop(1, rows, wait_o, 0)
    go_ref[...] = orecv[...]


def weight_kernel(per_step, wide, idx_ref, cnt_ref, og_ref, x_ref, out_ref):
    i = pl.program_id(0)
    base = pl.program_id(1) * per_step
    count = cnt_ref[i]
    blk = out_ref.shape[-1]
    x = x_ref[0]
    for s in range(0, per_step, wide):
        parts = []
        for m in range(wide):
            slot = base + s + m
            part = og_ref[idx_ref[i, slot]]
            parts.append(jnp.where(slot < count, part, jnp.zeros_like(part)))
        panel = jnp.concatenate(parts, axis=1)
        out = jnp.dot(x, panel, preferred_element_type=jnp.float32).astype(out_ref.dtype)
        for m in range(wide):
            out_ref[0, s + m] = out[:, m * blk : (m + 1) * blk]


def local(rows, activations, out_grad, weights, counts, col_index):
    blk = weights.shape[-1]
    here, slots = weights.shape[:2]
    tok, width = out_grad.shape
    act_tok = activations.shape[0]
    n_cols = width // blk
    tokens = rows * tok
    half = rows // 2
    chunks = n_cols // (2 * GROUP)
    bf16, f32 = jnp.bfloat16, jnp.float32

    index = col_index - lax.axis_index("col") * n_cols
    flat_slot = lax.broadcasted_iota(jnp.int32, (here, slots), 0) * slots
    slot_id = lax.broadcasted_iota(jnp.int32, (here, slots), 1)
    alive = slot_id < counts
    named = jnp.where(alive, index, -1)
    match = named[:, :, None] == lax.broadcasted_iota(jnp.int32, (1, 1, n_cols), 2)
    inverse = jnp.min(
        jnp.where(match, (flat_slot + slot_id)[:, :, None], here * slots), axis=1
    ).astype(jnp.int32)

    x_rows = -(-here * act_tok // 16) * 16
    xs = activations.reshape(act_tok, rows, here, blk).transpose(1, 2, 0, 3)
    xs = xs.reshape(rows, here * act_tok, blk)
    if x_rows != here * act_tok:
        xs = jnp.pad(xs, ((0, 0), (0, x_rows - here * act_tok), (0, 0)))

    here4 = -(-here // 4) * 4
    o_rows = here4 * 4
    q_shape = (rows, here4 // 2, 8, blk)
    vmem = pl.BlockSpec(memory_space=pltpu.VMEM)
    planned = (
        2 * (width * tokens * 2)
        + (here * slots + 1) * blk * blk * 2
        + tok * width * 4
        + 3 * 4 * rows * here4 * 4 * blk
        + 6 * 2 * rows * (2 * x_rows + o_rows) * blk
        + here * blk * max(tokens, 128) * 4
    )
    nat, x_all, g_all = pl.pallas_call(
        functools.partial(gather_kernel, rows, chunks),
        out_shape=(
            jax.ShapeDtypeStruct((n_cols, tokens, blk), bf16),
            jax.ShapeDtypeStruct((rows * 2, x_rows, blk), bf16),
            jax.ShapeDtypeStruct((rows, o_rows, blk), bf16),
        ),
        in_specs=[
            pl.BlockSpec(memory_space=pltpu.SMEM),
            vmem,
            vmem,
            pl.BlockSpec(memory_space=pl.ANY),
        ],
        out_specs=(vmem, vmem, vmem),
        scratch_shapes=[
            pltpu.VMEM((rows, n_cols // 2, 2 * tok, blk), bf16),
            pltpu.VMEM((here * slots + 1, blk, blk), bf16),
            pltpu.VMEM((here, blk, tokens), f32),
            pltpu.VMEM((rows * 2, x_rows, blk), bf16),
            pltpu.VMEM(q_shape, f32),
            pltpu.VMEM(q_shape, f32),
            pltpu.VMEM(q_shape, f32),
            pltpu.VMEM((rows, o_rows, blk), bf16),
            pltpu.VMEM((rows, o_rows, blk), bf16),
            pltpu.SemaphoreType.DMA,
            pltpu.SemaphoreType.DMA((2, half, chunks)),
            pltpu.SemaphoreType.DMA((2, half, chunks)),
            pltpu.SemaphoreType.DMA((rows * 2,)),
            pltpu.SemaphoreType.DMA((rows * 2,)),
            pltpu.SemaphoreType.DMA((2,)),
            pltpu.SemaphoreType.DMA((rows,)),
            pltpu.SemaphoreType.DMA((rows,)),
        ],
        compiler_params=pltpu.CompilerParams(
            collective_id=0,
            has_side_effects=True,
            vmem_limit_bytes=min(planned + (6 << 20), 60 << 20),
        ),
        cost_estimate=pl.CostEstimate(
            flops=2 * here * n_cols * blk * blk * tokens,
            bytes_accessed=weights.size * 2 + 2 * width * tokens * 2,
            transcendentals=0,
        ),
    )(inverse, out_grad, xs, weights.reshape(here * slots, blk, blk))

    x_t = x_all[:, : here * act_tok].reshape(rows * 2, here, act_tok, blk)
    x_t = x_t.transpose(1, 3, 0, 2).reshape(here, blk, tokens)

    per_step, wide = min(32, slots), 4
    grad_weight = pl.pallas_call(
        functools.partial(weight_kernel, per_step, wide),
        out_shape=jax.ShapeDtypeStruct(weights.shape, bf16),
        grid_spec=pltpu.PrefetchScalarGridSpec(
            num_scalar_prefetch=2,
            grid=(here, slots // per_step),
            in_specs=[
                pl.BlockSpec(
                    (n_cols, tokens, blk),
                    lambda i, j, *_: (0, 0, 0),
                    pipeline_mode=pl.Buffered(1),
                ),
                pl.BlockSpec((1, blk, tokens), lambda i, j, *_: (i, 0, 0)),
            ],
            out_specs=pl.BlockSpec((1, per_step, blk, blk), lambda i, j, *_: (i, j, 0, 0)),
        ),
        compiler_params=pltpu.CompilerParams(
            vmem_limit_bytes=n_cols * tokens * blk * 2 + (16 << 20),
        ),
    )(index, counts.reshape(here), nat, x_t)

    g = g_all[:, : here * act_tok].reshape(rows, here, act_tok, blk)
    grad_input = g.transpose(2, 0, 1, 3).reshape(act_tok, rows * here * blk)
    return grad_input, grad_weight


def solution(mesh):
    return jax.shard_map(
        functools.partial(local, mesh.shape["row"]),
        mesh=mesh,
        in_specs=(
            P(("grp", "row", "col"), None),
            P(("grp", "row"), "col"),
            P("row", "col", None, None),
            P("row", "col"),
            P("row", "col"),
        ),
        out_specs=(P(("grp", "row", "col"), None), P(("grp", "row"), "col", None, None)),
        check_vma=False,
    )
```

```python
import functools

import jax
import jax.numpy as jnp
from jax import lax
from jax.experimental import pallas as pl
from jax.experimental.pallas import tpu as pltpu
from jax.sharding import PartitionSpec as P

MESH = pl.DeviceIdType.MESH
GROUP = 8
AHEAD = 2


def gather_kernel(
    rows,
    chunks,
    inv_ref,
    og_ref,
    xs_ref,
    w_hbm,
    nat_ref,
    xo_ref,
    go_ref,
    raw,
    wbuf,
    acc,
    xr,
    q_send,
    q_recv,
    q_mine,
    obuf,
    orecv,
    w_sem,
    ring_send,
    ring_recv,
    x_send,
    x_recv,
    q_sems,
    o_send,
    o_recv,
):
    half = rows // 2
    here = acc.shape[0]
    slots = w_hbm.shape[0]
    blk = w_hbm.shape[-1]
    tok = og_ref.shape[0]
    tokens = rows * tok
    pairs = raw.shape[1] // chunks
    cols = pairs * 2
    peers = rows * 2
    row = lax.axis_index("row")
    col = lax.axis_index("col")
    me = row * 2 + col
    odd = row % 2
    pos = (1 - odd) * (row // 2) + odd * (rows - 1 - row // 2)

    def row_at(p):
        p = (p + 2 * rows) % rows
        hi = p // half
        return (1 - hi) * (2 * p) + hi * (2 * (rows - 1 - p) + 1)

    barrier = pltpu.get_barrier_semaphore()

    def greet(d, _):
        peer = (me + d) % peers
        pl.semaphore_signal(
            barrier, inc=1, device_id={"row": peer // 2, "col": peer % 2}, device_id_type=MESH
        )
        return 0

    lax.fori_loop(1, peers, greet, 0)
    w_copy = pltpu.make_async_copy(w_hbm, wbuf.at[pl.ds(0, slots)], w_sem)
    w_copy.start()

    def lay_out(q, _):
        both = og_ref[:, pl.ds(pl.multiple_of(q * 2 * blk, 2 * blk), 2 * blk)].astype(jnp.float32)
        raw[row, q] = jnp.concatenate([both[:, :blk], both[:, blk:]], axis=0).astype(raw.dtype)
        return 0

    lax.fori_loop(0, raw.shape[1], lay_out, 0, unroll=4)
    pl.semaphore_wait(barrier, peers - 1)

    def ring_copy(d, k, c):
        origin = row_at(pos - k) if d == 0 else row_at(pos + k)
        target = row_at(pos + 1) if d == 0 else row_at(pos - 1)
        part = raw.at[origin, pl.ds(c * pairs, pairs)]
        return pltpu.make_async_remote_copy(
            src_ref=part,
            dst_ref=part,
            send_sem=ring_send.at[d, k, c],
            recv_sem=ring_recv.at[d, k, c],
            device_id={"row": target},
            device_id_type=MESH,
        )

    def ring_arrival(d, k, c):
        origin = row_at(pos - 1 - k) if d == 0 else row_at(pos + 1 + k)
        target = row_at(pos + 1) if d == 0 else row_at(pos - 1)
        part = raw.at[origin, pl.ds(c * pairs, pairs)]
        return pltpu.make_async_remote_copy(
            src_ref=part,
            dst_ref=part,
            send_sem=ring_send.at[d, k, c],
            recv_sem=ring_recv.at[d, k, c],
            device_id={"row": target},
            device_id_type=MESH,
        )

    def x_copy(d):
        peer = (me + d) % peers
        return pltpu.make_async_remote_copy(
            src_ref=xs_ref.at[peer // 2],
            dst_ref=xr.at[me],
            send_sem=x_send.at[d],
            recv_sem=x_recv.at[d],
            device_id={"row": peer // 2, "col": peer % 2},
            device_id_type=MESH,
        )

    def x_arrival(d):
        peer = (me + peers - d) % peers
        return pltpu.make_async_remote_copy(
            src_ref=xs_ref.at[peer // 2],
            dst_ref=xr.at[peer],
            send_sem=x_send.at[d],
            recv_sem=x_recv.at[d],
            device_id={"row": peer // 2, "col": peer % 2},
            device_id_type=MESH,
        )

    for c in range(min(AHEAD, chunks)):
        for d in (0, 1):
            ring_copy(d, 0, c).start()

    def send_x(d, _):
        x_copy(d).start()
        return 0

    lax.fori_loop(1, peers, send_x, 0)
    xr[me] = xs_ref[row]
    wbuf[slots] = jnp.zeros((blk, blk), wbuf.dtype)
    acc[...] = jnp.zeros_like(acc)

    def hop(t, k):
        c = t - k
        for d in (0, 1):
            ok = (c >= 0) & (c < chunks)
            if k == half - 1:
                ok = ok & (c % 2 == d)

            @pl.when(ok)
            def _():
                ring_arrival(d, k - 1, c).wait_recv()
                ring_copy(d, k, c).start()

    def compute(c):
        def natural(j, _):
            q = c * pairs + j
            both = raw[:, q].astype(jnp.float32).reshape(rows, 2, tok, blk)
            nat_ref[2 * q] = both[:, 0].reshape(tokens, blk).astype(nat_ref.dtype)
            nat_ref[2 * q + 1] = both[:, 1].reshape(tokens, blk).astype(nat_ref.dtype)
            return 0

        lax.fori_loop(0, pairs, natural, 0, unroll=2)

        def group(g, _):
            first = c * cols + g * GROUP
            panel = jnp.concatenate([nat_ref[first + m] for m in range(GROUP)], axis=1)
            for i in range(here):
                blocks = jnp.concatenate(
                    [wbuf[inv_ref[i, first + m]] for m in range(GROUP)], axis=1
                )
                acc[i] += lax.dot_general(
                    blocks, panel, (((1,), (1,)), ((), ())), preferred_element_type=jnp.float32
                )
            return 0

        lax.fori_loop(0, cols // GROUP, group, 0)

    def tick(t, _):
        @pl.when(t + AHEAD < chunks)
        def _():
            for d in (0, 1):
                ring_copy(d, 0, t + AHEAD).start()

        if half > 1:
            hop(t, 1)
        for k in range(half - 1, 1, -1):
            hop(t, k)

        @pl.when(t >= half)
        def _():
            c = t - half

            @pl.when(c == 0)
            def _():
                w_copy.wait()

            for d in (0, 1):
                @pl.when(c % 2 == d)
                def _():
                    ring_arrival(d, half - 1, c).wait_recv()
                    ring_arrival(1 - d, half - 2, c).wait_recv()

            compute(c)

        return 0

    lax.fori_loop(0, chunks + half, tick, 0)

    below = lax.broadcasted_iota(jnp.int32, (rows, 8, blk), 1) < 4
    first_core = (lax.broadcasted_iota(jnp.int32, (rows, 8, blk), 1) * 0 + col) == 0
    zero = jnp.zeros((rows, 8, blk), jnp.float32)

    def tile(i):
        if i >= here:
            return zero
        return jnp.transpose(acc[i], (1, 0)).reshape(rows, tok, blk)

    for i2 in range(q_send.shape[1]):
        a, b = tile(2 * i2), tile(2 * i2 + 1)
        for_first = jnp.where(below, a, pltpu.roll(b, 4, 1))
        for_second = jnp.where(below, pltpu.roll(a, 4, 1), b)
        q_mine[:, i2] = jnp.where(first_core, for_first, for_second)
        q_send[:, i2] = jnp.where(first_core, for_second, for_first)

    swap = pltpu.make_async_remote_copy(
        src_ref=q_send,
        dst_ref=q_recv,
        send_sem=q_sems.at[0],
        recv_sem=q_sems.at[1],
        device_id={"col": 1 - col},
        device_id_type=MESH,
    )
    swap.start()

    def wait_x(d, _):
        x_arrival(d).wait_recv()
        x_copy(d).wait_send()
        return 0

    lax.fori_loop(1, peers, wait_x, 0)
    xo_ref[...] = xr[...]

    def wait_ring(c, _):
        for k in range(half):
            for d in (0, 1):
                if k == half - 1:

                    @pl.when(c % 2 == d)
                    def _():
                        ring_copy(d, k, c).wait_send()

                else:
                    ring_copy(d, k, c).wait_send()
        return 0

    lax.fori_loop(0, chunks, wait_ring, 0)
    swap.wait()
    total = q_mine[...] + q_recv[...]
    obuf[...] = total.reshape(obuf.shape).astype(obuf.dtype)

    def o_copy(d):
        peer = (row + d) % rows
        return pltpu.make_async_remote_copy(
            src_ref=obuf.at[peer],
            dst_ref=orecv.at[row],
            send_sem=o_send.at[d],
            recv_sem=o_recv.at[d],
            device_id={"row": peer},
            device_id_type=MESH,
        )

    def o_arrival(d):
        peer = (row + rows - d) % rows
        return pltpu.make_async_remote_copy(
            src_ref=obuf.at[peer],
            dst_ref=orecv.at[peer],
            send_sem=o_send.at[d],
            recv_sem=o_recv.at[d],
            device_id={"row": peer},
            device_id_type=MESH,
        )

    def send_o(d, _):
        o_copy(d).start()
        return 0

    def wait_o(d, _):
        o_arrival(d).wait_recv()
        o_copy(d).wait_send()
        return 0

    lax.fori_loop(1, rows, send_o, 0)
    orecv[row] = obuf[row]
    lax.fori_loop(1, rows, wait_o, 0)
    go_ref[...] = orecv[...]


def weight_kernel(per_step, wide, depth, idx_ref, cnt_ref, og_ref, x_ref, out_hbm, buf, sems):
    here, slots = out_hbm.shape[:2]
    blk = out_hbm.shape[-1]
    per_row = slots // per_step
    steps = here * per_row

    def out_copy(t):
        lane = t % depth
        return pltpu.make_async_copy(
            buf.at[lane],
            out_hbm.at[t // per_row, pl.ds((t % per_row) * per_step, per_step)],
            sems.at[lane],
        )

    def step(t, _):
        i = t // per_row
        base = (t % per_row) * per_step
        lane = t % depth
        count = cnt_ref[i]
        x = x_ref[i]

        @pl.when(t >= depth)
        def _():
            out_copy(t - depth).wait()

        for s in range(0, per_step, wide):
            parts = []
            for m in range(wide):
                slot = base + s + m
                part = og_ref[idx_ref[i, slot]]
                parts.append(jnp.where(slot < count, part, jnp.zeros_like(part)))
            panel = jnp.concatenate(parts, axis=1)
            out = jnp.dot(x, panel, preferred_element_type=jnp.float32).astype(buf.dtype)
            for m in range(wide):
                buf[lane, s + m] = out[:, m * blk : (m + 1) * blk]
        out_copy(t).start()
        return 0

    lax.fori_loop(0, steps, step, 0)
    for t in range(max(0, steps - depth), steps):
        out_copy(t).wait()


def local(rows, activations, out_grad, weights, counts, col_index):
    blk = weights.shape[-1]
    here, slots = weights.shape[:2]
    tok, width = out_grad.shape
    act_tok = activations.shape[0]
    n_cols = width // blk
    tokens = rows * tok
    half = rows // 2
    chunks = n_cols // (4 * GROUP)
    bf16, f32 = jnp.bfloat16, jnp.float32

    index = col_index - lax.axis_index("col") * n_cols
    flat_slot = lax.broadcasted_iota(jnp.int32, (here, slots), 0) * slots
    slot_id = lax.broadcasted_iota(jnp.int32, (here, slots), 1)
    alive = slot_id < counts
    named = jnp.where(alive, index, -1)
    match = named[:, :, None] == lax.broadcasted_iota(jnp.int32, (1, 1, n_cols), 2)
    inverse = jnp.min(
        jnp.where(match, (flat_slot + slot_id)[:, :, None], here * slots), axis=1
    ).astype(jnp.int32)

    x_rows = -(-here * act_tok // 16) * 16
    xs = activations.reshape(act_tok, rows, here, blk).transpose(1, 2, 0, 3)
    xs = xs.reshape(rows, here * act_tok, blk)
    if x_rows != here * act_tok:
        xs = jnp.pad(xs, ((0, 0), (0, x_rows - here * act_tok), (0, 0)))

    here4 = -(-here // 4) * 4
    o_rows = here4 * 4
    q_shape = (rows, here4 // 2, 8, blk)
    vmem = pl.BlockSpec(memory_space=pltpu.VMEM)
    planned = (
        2 * (width * tokens * 2)
        + (here * slots + 1) * blk * blk * 2
        + tok * width * 4
        + 3 * 4 * rows * here4 * 4 * blk
        + 6 * 2 * rows * (2 * x_rows + o_rows) * blk
        + here * blk * max(tokens, 128) * 4
    )
    nat, x_all, g_all = pl.pallas_call(
        functools.partial(gather_kernel, rows, chunks),
        out_shape=(
            jax.ShapeDtypeStruct((n_cols, tokens, blk), bf16),
            jax.ShapeDtypeStruct((rows * 2, x_rows, blk), bf16),
            jax.ShapeDtypeStruct((rows, o_rows, blk), bf16),
        ),
        in_specs=[
            pl.BlockSpec(memory_space=pltpu.SMEM),
            vmem,
            vmem,
            pl.BlockSpec(memory_space=pl.ANY),
        ],
        out_specs=(vmem, vmem, vmem),
        scratch_shapes=[
            pltpu.VMEM((rows, n_cols // 2, 2 * tok, blk), bf16),
            pltpu.VMEM((here * slots + 1, blk, blk), bf16),
            pltpu.VMEM((here, blk, tokens), f32),
            pltpu.VMEM((rows * 2, x_rows, blk), bf16),
            pltpu.VMEM(q_shape, f32),
            pltpu.VMEM(q_shape, f32),
            pltpu.VMEM(q_shape, f32),
            pltpu.VMEM((rows, o_rows, blk), bf16),
            pltpu.VMEM((rows, o_rows, blk), bf16),
            pltpu.SemaphoreType.DMA,
            pltpu.SemaphoreType.DMA((2, half, chunks)),
            pltpu.SemaphoreType.DMA((2, half, chunks)),
            pltpu.SemaphoreType.DMA((rows * 2,)),
            pltpu.SemaphoreType.DMA((rows * 2,)),
            pltpu.SemaphoreType.DMA((2,)),
            pltpu.SemaphoreType.DMA((rows,)),
            pltpu.SemaphoreType.DMA((rows,)),
        ],
        compiler_params=pltpu.CompilerParams(
            collective_id=0,
            has_side_effects=True,
            vmem_limit_bytes=min(planned + (6 << 20), 60 << 20),
        ),
        cost_estimate=pl.CostEstimate(
            flops=2 * here * n_cols * blk * blk * tokens,
            bytes_accessed=weights.size * 2 + 2 * width * tokens * 2,
            transcendentals=0,
        ),
    )(inverse, out_grad, xs, weights.reshape(here * slots, blk, blk))

    x_t = x_all[:, : here * act_tok].reshape(rows * 2, here, act_tok, blk)
    x_t = x_t.transpose(1, 3, 0, 2).reshape(here, blk, tokens)

    per_step, wide, depth = min(128, slots), 8, 2
    grad_weight = pl.pallas_call(
        functools.partial(weight_kernel, per_step, wide, depth),
        out_shape=jax.ShapeDtypeStruct(weights.shape, bf16),
        in_specs=[
            pl.BlockSpec(memory_space=pltpu.SMEM),
            pl.BlockSpec(memory_space=pltpu.SMEM),
            vmem,
            vmem,
        ],
        out_specs=pl.BlockSpec(memory_space=pl.ANY),
        scratch_shapes=[
            pltpu.VMEM((depth, per_step, blk, blk), bf16),
            pltpu.SemaphoreType.DMA((depth,)),
        ],
        compiler_params=pltpu.CompilerParams(
            vmem_limit_bytes=n_cols * tokens * blk * 2 + (16 << 20),
        ),
    )(index, counts.reshape(here), nat, x_t)

    g = g_all[:, : here * act_tok].reshape(rows, here, act_tok, blk)
    grad_input = g.transpose(2, 0, 1, 3).reshape(act_tok, rows * here * blk)
    return grad_input, grad_weight


def solution(mesh):
    return jax.shard_map(
        functools.partial(local, mesh.shape["row"]),
        mesh=mesh,
        in_specs=(
            P(("grp", "row", "col"), None),
            P(("grp", "row"), "col"),
            P("row", "col", None, None),
            P("row", "col"),
            P("row", "col"),
        ),
        out_specs=(P(("grp", "row", "col"), None), P(("grp", "row"), "col", None, None)),
        check_vma=False,
    )
```

```python
import functools

import jax
import jax.numpy as jnp
from jax import lax
from jax.experimental import pallas as pl
from jax.experimental.pallas import tpu as pltpu
from jax.sharding import PartitionSpec as P

MESH = pl.DeviceIdType.MESH
GROUP = 8
AHEAD = 1


def gather_kernel(
    rows,
    chunks,
    inv_ref,
    og_ref,
    xs_ref,
    w_hbm,
    nat_ref,
    xo_ref,
    go_ref,
    raw,
    wbuf,
    acc,
    xr,
    q_send,
    q_recv,
    q_mine,
    obuf,
    orecv,
    w_sem,
    ring_send,
    ring_recv,
    x_send,
    x_recv,
    q_sems,
    o_send,
    o_recv,
):
    half = rows // 2
    here = acc.shape[0]
    slots = w_hbm.shape[0]
    blk = w_hbm.shape[-1]
    tok = og_ref.shape[0]
    tokens = rows * tok
    pairs = raw.shape[1] // chunks
    cols = pairs * 2
    peers = rows * 2
    row = lax.axis_index("row")
    col = lax.axis_index("col")
    me = row * 2 + col
    odd = row % 2
    pos = (1 - odd) * (row // 2) + odd * (rows - 1 - row // 2)

    def row_at(p):
        p = (p + 2 * rows) % rows
        hi = p // half
        return (1 - hi) * (2 * p) + hi * (2 * (rows - 1 - p) + 1)

    barrier = pltpu.get_barrier_semaphore()

    def greet(d, _):
        peer = (me + d) % peers
        pl.semaphore_signal(
            barrier, inc=1, device_id={"row": peer // 2, "col": peer % 2}, device_id_type=MESH
        )
        return 0

    lax.fori_loop(1, peers, greet, 0)
    w_copy = pltpu.make_async_copy(w_hbm, wbuf.at[pl.ds(0, slots)], w_sem)
    w_copy.start()

    def lay_out(q, _):
        both = og_ref[:, pl.ds(pl.multiple_of(q * 2 * blk, 2 * blk), 2 * blk)].astype(jnp.float32)
        raw[row, q] = jnp.concatenate([both[:, :blk], both[:, blk:]], axis=0).astype(raw.dtype)
        return 0

    lax.fori_loop(0, raw.shape[1], lay_out, 0, unroll=4)
    pl.semaphore_wait(barrier, peers - 1)

    def ring_copy(d, k, c):
        origin = row_at(pos - k) if d == 0 else row_at(pos + k)
        target = row_at(pos + 1) if d == 0 else row_at(pos - 1)
        part = raw.at[origin, pl.ds(c * pairs, pairs)]
        return pltpu.make_async_remote_copy(
            src_ref=part,
            dst_ref=part,
            send_sem=ring_send.at[d, k, c],
            recv_sem=ring_recv.at[d, k, c],
            device_id={"row": target},
            device_id_type=MESH,
        )

    def ring_arrival(d, k, c):
        origin = row_at(pos - 1 - k) if d == 0 else row_at(pos + 1 + k)
        target = row_at(pos + 1) if d == 0 else row_at(pos - 1)
        part = raw.at[origin, pl.ds(c * pairs, pairs)]
        return pltpu.make_async_remote_copy(
            src_ref=part,
            dst_ref=part,
            send_sem=ring_send.at[d, k, c],
            recv_sem=ring_recv.at[d, k, c],
            device_id={"row": target},
            device_id_type=MESH,
        )

    def x_copy(d):
        peer = (me + d) % peers
        return pltpu.make_async_remote_copy(
            src_ref=xs_ref.at[peer // 2],
            dst_ref=xr.at[me],
            send_sem=x_send.at[d],
            recv_sem=x_recv.at[d],
            device_id={"row": peer // 2, "col": peer % 2},
            device_id_type=MESH,
        )

    def x_arrival(d):
        peer = (me + peers - d) % peers
        return pltpu.make_async_remote_copy(
            src_ref=xs_ref.at[peer // 2],
            dst_ref=xr.at[peer],
            send_sem=x_send.at[d],
            recv_sem=x_recv.at[d],
            device_id={"row": peer // 2, "col": peer % 2},
            device_id_type=MESH,
        )

    for c in range(min(AHEAD, chunks)):
        for d in (0, 1):
            ring_copy(d, 0, c).start()

    def send_x(d, _):
        x_copy(d).start()
        return 0

    lax.fori_loop(1, peers, send_x, 0)
    xr[me] = xs_ref[row]
    wbuf[slots] = jnp.zeros((blk, blk), wbuf.dtype)
    acc[...] = jnp.zeros_like(acc)

    def hop(t, k):
        c = t - k
        for d in (0, 1):
            ok = (c >= 0) & (c < chunks)
            if k == half - 1:
                ok = ok & (c % 2 == d)

            @pl.when(ok)
            def _():
                ring_arrival(d, k - 1, c).wait_recv()
                ring_copy(d, k, c).start()

    def compute(c):
        def natural(j, _):
            q = c * pairs + j
            both = raw[:, q].astype(jnp.float32).reshape(rows, 2, tok, blk)
            nat_ref[2 * q] = both[:, 0].reshape(tokens, blk).astype(nat_ref.dtype)
            nat_ref[2 * q + 1] = both[:, 1].reshape(tokens, blk).astype(nat_ref.dtype)
            return 0

        lax.fori_loop(0, pairs, natural, 0, unroll=2)

        def group(g, _):
            first = c * cols + g * GROUP
            panel = jnp.concatenate([nat_ref[first + m] for m in range(GROUP)], axis=1)
            for i in range(here):
                blocks = jnp.concatenate(
                    [wbuf[inv_ref[i, first + m]] for m in range(GROUP)], axis=1
                )
                acc[i] += lax.dot_general(
                    blocks, panel, (((1,), (1,)), ((), ())), preferred_element_type=jnp.float32
                )
            return 0

        lax.fori_loop(0, cols // GROUP, group, 0)

    def tick(t, _):
        @pl.when(t + AHEAD < chunks)
        def _():
            for d in (0, 1):
                ring_copy(d, 0, t + AHEAD).start()

        if half > 1:
            hop(t, 1)
        for k in range(half - 1, 1, -1):
            hop(t, k)

        @pl.when(t >= half)
        def _():
            c = t - half

            @pl.when(c == 0)
            def _():
                w_copy.wait()

            for d in (0, 1):
                @pl.when(c % 2 == d)
                def _():
                    ring_arrival(d, half - 1, c).wait_recv()
                    ring_arrival(1 - d, half - 2, c).wait_recv()

            compute(c)

        return 0

    lax.fori_loop(0, chunks + half, tick, 0)

    below = lax.broadcasted_iota(jnp.int32, (rows, 8, blk), 1) < 4
    first_core = (lax.broadcasted_iota(jnp.int32, (rows, 8, blk), 1) * 0 + col) == 0
    zero = jnp.zeros((rows, 8, blk), jnp.float32)

    def tile(i):
        if i >= here:
            return zero
        return jnp.transpose(acc[i], (1, 0)).reshape(rows, tok, blk)

    for i2 in range(q_send.shape[1]):
        a, b = tile(2 * i2), tile(2 * i2 + 1)
        for_first = jnp.where(below, a, pltpu.roll(b, 4, 1))
        for_second = jnp.where(below, pltpu.roll(a, 4, 1), b)
        q_mine[:, i2] = jnp.where(first_core, for_first, for_second)
        q_send[:, i2] = jnp.where(first_core, for_second, for_first)

    swap = pltpu.make_async_remote_copy(
        src_ref=q_send,
        dst_ref=q_recv,
        send_sem=q_sems.at[0],
        recv_sem=q_sems.at[1],
        device_id={"col": 1 - col},
        device_id_type=MESH,
    )
    swap.start()

    def wait_x(d, _):
        x_arrival(d).wait_recv()
        x_copy(d).wait_send()
        return 0

    lax.fori_loop(1, peers, wait_x, 0)
    xo_ref[...] = xr[...]

    def wait_ring(c, _):
        for k in range(half):
            for d in (0, 1):
                if k == half - 1:

                    @pl.when(c % 2 == d)
                    def _():
                        ring_copy(d, k, c).wait_send()

                else:
                    ring_copy(d, k, c).wait_send()
        return 0

    lax.fori_loop(0, chunks, wait_ring, 0)
    swap.wait()
    total = q_mine[...] + q_recv[...]
    obuf[...] = total.reshape(obuf.shape).astype(obuf.dtype)

    def o_copy(d):
        peer = (row + d) % rows
        return pltpu.make_async_remote_copy(
            src_ref=obuf.at[peer],
            dst_ref=orecv.at[row],
            send_sem=o_send.at[d],
            recv_sem=o_recv.at[d],
            device_id={"row": peer},
            device_id_type=MESH,
        )

    def o_arrival(d):
        peer = (row + rows - d) % rows
        return pltpu.make_async_remote_copy(
            src_ref=obuf.at[peer],
            dst_ref=orecv.at[peer],
            send_sem=o_send.at[d],
            recv_sem=o_recv.at[d],
            device_id={"row": peer},
            device_id_type=MESH,
        )

    def send_o(d, _):
        o_copy(d).start()
        return 0

    def wait_o(d, _):
        o_arrival(d).wait_recv()
        o_copy(d).wait_send()
        return 0

    lax.fori_loop(1, rows, send_o, 0)
    orecv[row] = obuf[row]
    lax.fori_loop(1, rows, wait_o, 0)
    go_ref[...] = orecv[...]


def weight_kernel(per_step, wide, depth, idx_ref, cnt_ref, og_ref, x_ref, out_hbm, buf, sems):
    here, slots = out_hbm.shape[:2]
    blk = out_hbm.shape[-1]
    per_row = slots // per_step
    steps = here * per_row

    def out_copy(t):
        lane = t % depth
        return pltpu.make_async_copy(
            buf.at[lane],
            out_hbm.at[t // per_row, pl.ds((t % per_row) * per_step, per_step)],
            sems.at[lane],
        )

    def step(t, _):
        i = t // per_row
        base = (t % per_row) * per_step
        lane = t % depth
        count = cnt_ref[i]
        x = x_ref[i]

        @pl.when(t >= depth)
        def _():
            out_copy(t - depth).wait()

        for s in range(0, per_step, wide):
            parts = []
            for m in range(wide):
                slot = base + s + m
                part = og_ref[idx_ref[i, slot]]
                parts.append(jnp.where(slot < count, part, jnp.zeros_like(part)))
            panel = jnp.concatenate(parts, axis=1)
            out = jnp.dot(x, panel, preferred_element_type=jnp.float32).astype(buf.dtype)
            for m in range(wide):
                buf[lane, s + m] = out[:, m * blk : (m + 1) * blk]
        out_copy(t).start()
        return 0

    lax.fori_loop(0, steps, step, 0)
    for t in range(max(0, steps - depth), steps):
        out_copy(t).wait()


def local(rows, activations, out_grad, weights, counts, col_index):
    blk = weights.shape[-1]
    here, slots = weights.shape[:2]
    tok, width = out_grad.shape
    act_tok = activations.shape[0]
    n_cols = width // blk
    tokens = rows * tok
    half = rows // 2
    chunks = n_cols // (4 * GROUP)
    bf16, f32 = jnp.bfloat16, jnp.float32

    index = col_index - lax.axis_index("col") * n_cols
    flat_slot = lax.broadcasted_iota(jnp.int32, (here, slots), 0) * slots
    slot_id = lax.broadcasted_iota(jnp.int32, (here, slots), 1)
    alive = slot_id < counts
    named = jnp.where(alive, index, -1)
    match = named[:, :, None] == lax.broadcasted_iota(jnp.int32, (1, 1, n_cols), 2)
    inverse = jnp.min(
        jnp.where(match, (flat_slot + slot_id)[:, :, None], here * slots), axis=1
    ).astype(jnp.int32)

    x_rows = -(-here * act_tok // 16) * 16
    xs = activations.reshape(act_tok, rows, here, blk).transpose(1, 2, 0, 3)
    xs = xs.reshape(rows, here * act_tok, blk)
    if x_rows != here * act_tok:
        xs = jnp.pad(xs, ((0, 0), (0, x_rows - here * act_tok), (0, 0)))

    here4 = -(-here // 4) * 4
    o_rows = here4 * 4
    q_shape = (rows, here4 // 2, 8, blk)
    vmem = pl.BlockSpec(memory_space=pltpu.VMEM)
    planned = (
        2 * (width * tokens * 2)
        + (here * slots + 1) * blk * blk * 2
        + tok * width * 4
        + 3 * 4 * rows * here4 * 4 * blk
        + 6 * 2 * rows * (2 * x_rows + o_rows) * blk
        + here * blk * max(tokens, 128) * 4
    )
    nat, x_all, g_all = pl.pallas_call(
        functools.partial(gather_kernel, rows, chunks),
        out_shape=(
            jax.ShapeDtypeStruct((n_cols, tokens, blk), bf16),
            jax.ShapeDtypeStruct((rows * 2, x_rows, blk), bf16),
            jax.ShapeDtypeStruct((rows, o_rows, blk), bf16),
        ),
        in_specs=[
            pl.BlockSpec(memory_space=pltpu.SMEM),
            vmem,
            vmem,
            pl.BlockSpec(memory_space=pl.ANY),
        ],
        out_specs=(vmem, vmem, vmem),
        scratch_shapes=[
            pltpu.VMEM((rows, n_cols // 2, 2 * tok, blk), bf16),
            pltpu.VMEM((here * slots + 1, blk, blk), bf16),
            pltpu.VMEM((here, blk, tokens), f32),
            pltpu.VMEM((rows * 2, x_rows, blk), bf16),
            pltpu.VMEM(q_shape, f32),
            pltpu.VMEM(q_shape, f32),
            pltpu.VMEM(q_shape, f32),
            pltpu.VMEM((rows, o_rows, blk), bf16),
            pltpu.VMEM((rows, o_rows, blk), bf16),
            pltpu.SemaphoreType.DMA,
            pltpu.SemaphoreType.DMA((2, half, chunks)),
            pltpu.SemaphoreType.DMA((2, half, chunks)),
            pltpu.SemaphoreType.DMA((rows * 2,)),
            pltpu.SemaphoreType.DMA((rows * 2,)),
            pltpu.SemaphoreType.DMA((2,)),
            pltpu.SemaphoreType.DMA((rows,)),
            pltpu.SemaphoreType.DMA((rows,)),
        ],
        compiler_params=pltpu.CompilerParams(
            collective_id=0,
            has_side_effects=True,
            vmem_limit_bytes=min(planned + (6 << 20), 60 << 20),
        ),
        cost_estimate=pl.CostEstimate(
            flops=2 * here * n_cols * blk * blk * tokens,
            bytes_accessed=weights.size * 2 + 2 * width * tokens * 2,
            transcendentals=0,
        ),
    )(inverse, out_grad, xs, weights.reshape(here * slots, blk, blk))

    x_t = x_all[:, : here * act_tok].reshape(rows * 2, here, act_tok, blk)
    x_t = x_t.transpose(1, 3, 0, 2).reshape(here, blk, tokens)

    per_step, wide, depth = min(128, slots), 8, 2
    grad_weight = pl.pallas_call(
        functools.partial(weight_kernel, per_step, wide, depth),
        out_shape=jax.ShapeDtypeStruct(weights.shape, bf16),
        in_specs=[
            pl.BlockSpec(memory_space=pltpu.SMEM),
            pl.BlockSpec(memory_space=pltpu.SMEM),
            vmem,
            vmem,
        ],
        out_specs=pl.BlockSpec(memory_space=pl.ANY),
        scratch_shapes=[
            pltpu.VMEM((depth, per_step, blk, blk), bf16),
            pltpu.SemaphoreType.DMA((depth,)),
        ],
        compiler_params=pltpu.CompilerParams(
            vmem_limit_bytes=n_cols * tokens * blk * 2 + (16 << 20),
        ),
    )(index, counts.reshape(here), nat, x_t)

    g = g_all[:, : here * act_tok].reshape(rows, here, act_tok, blk)
    grad_input = g.transpose(2, 0, 1, 3).reshape(act_tok, rows * here * blk)
    return grad_input, grad_weight


def solution(mesh):
    return jax.shard_map(
        functools.partial(local, mesh.shape["row"]),
        mesh=mesh,
        in_specs=(
            P(("grp", "row", "col"), None),
            P(("grp", "row"), "col"),
            P("row", "col", None, None),
            P("row", "col"),
            P("row", "col"),
        ),
        out_specs=(P(("grp", "row", "col"), None), P(("grp", "row"), "col", None, None)),
        check_vma=False,
    )
```
